32 devices in a mesh: slab: 2 (over x), energy: 16 (over z, y, core).
Axes of the slice: x: 2, y: 2, z: 4, core: 2. Of those that a mesh axis runs over, the one named last changes fastest.
Arguments:
- retarded: float32 [2, 32, 2, 256, 256], P('slab', 'energy'), may hold values from -0.375 to 0.375
- lesser_prev: float32 [2, 32, 2, 256, 256], P('slab', 'energy'), may hold values from -1.8 to 1.8
- hopping: float32 [2, 256, 256], P('slab'), may hold values from -0.375 to 0.375
- hop_mask: int32 [2, 4, 4], P('slab'), may hold values 0 or 1
- offsets: int32 [3], replicated, may hold values from 1 to 6, as said below
- coupling: float32 [3], replicated, may hold values from 0.3 to 1
- occupation: float32 [3], replicated, may hold values from 0.1 to 3
Outputs:
- lesser: float32 [2, 32, 2, 256, 256], P('slab', 'energy')
The draws below stay inside these ranges and needn't reach their ends.
Inputs may be any that keep to these rules, and one draw needn't show every extreme that they name: `offsets`: the offset of mode k lies in k * 2 + 1 to (k + 1) * 2, and the last mode's equals 6.
All inputs are finite; a program needn't handle non-finite values. No bound on the sum of `hop_mask` on one device may be relied on, other than what follows from the above.
Results may differ from the reference program's by a relative error of at most 0.00014.
Values sent between devices are 32-bit elements; how exact they have to be, the bound alone decides.
No kernel may reach another device: no remote copies, remote signals or barrier semaphores. Data moves between devices by JAX's collectives and lax.ppermute only.
A program may use at most 64 MiB of HBM per device.

```python
import math
import jax
import jax.numpy as jnp
from jax import lax

B = 256
TILE = 64
E_DEV = 2
MODES = 3
QMAX = 6
NE = 32
SLABS = 2


def draw_offsets(key, part):
    mode_index = jnp.arange(MODES, dtype=jnp.int32)
    jitter = jax.random.randint(key, (MODES,), 0, E_DEV, dtype=jnp.int32)
    drawn = mode_index * E_DEV + 1 + jitter
    return jnp.where(mode_index == MODES - 1, MODES * E_DEV, drawn).astype(jnp.int32)


def place_ends(entries, stream_key, low, largest):
    spot = [jax.random.randint(jax.random.fold_in(stream_key, axis), (), 0, length) for axis, length in enumerate(entries.shape)]
    main_axis = entries.shape.index(max(entries.shape))
    beside = spot[:main_axis] + [(spot[main_axis] + 1) % entries.shape[main_axis]] + spot[main_axis + 1:]
    return entries.at[tuple(spot)].set(low).at[tuple(beside)].set(largest)


def steps_of(rng, shape, pieces, smallest, high):
    def one(position, parts):
        steps = jax.random.uniform(jax.random.fold_in(jax.random.fold_in(rng, 6), position), (parts,), jnp.float32, smallest / len(pieces), high / len(pieces))
        return jnp.repeat(jnp.exp(steps), shape[position] // parts).reshape((-1,) + (1,) * (len(shape) - position - 1))

    loudness = one(*pieces[0])
    for cut in pieces[1:]:
        loudness = loudness * one(*cut)
    return loudness


def scatter_about(stream_key, dims, scale, most, shards=(), kind=jnp.bfloat16):
    entries = jax.random.normal(stream_key, dims, jnp.float32) * scale
    if len(shards) > 0:
        entries = steps_of(stream_key, dims, shards, -0.22, 0.18) * entries
    return jnp.clip(entries, min=-most, max=most).astype(kind)


def setup_inputs(seed: int = 0) -> dict:
    streams_of = jax.random.split(jax.random.key(seed), 8)
    retarded = scatter_about(streams_of[0], (SLABS, NE, 2, B, B), B ** -0.5, 0.375, ((0, 2), (1, 16)), jnp.float32)
    lesser_prev = scatter_about(streams_of[1], (SLABS, NE, 2, B, B), 0.3, 1.8, ((0, 2), (1, 16)), jnp.float32)
    hopping = scatter_about(streams_of[2], (SLABS, B, B), B ** -0.5, 0.375, ((0, 2),), jnp.float32)
    hop_mask = place_ends((jax.random.randint(streams_of[3], (SLABS, B // TILE, B // TILE), 0, 2) < 1).astype(jnp.int32), jax.random.fold_in(streams_of[3], 1), 0, 1)
    offsets = draw_offsets(jax.random.fold_in(streams_of[7], 71), 0)
    coupling = jnp.clip(jnp.exp(jax.random.uniform(streams_of[5], (MODES,), jnp.float32, math.log(0.3), math.log(1.0))), 0.3, 1.0)
    occupation = jnp.clip(jnp.exp(jax.random.uniform(streams_of[6], (MODES,), jnp.float32, math.log(0.1), math.log(3.0))), 0.1, 3.0)
    return dict(retarded=retarded, lesser_prev=lesser_prev, hopping=hopping, hop_mask=hop_mask, offsets=offsets, coupling=coupling, occupation=occupation)


def matmul_high(left_matrix, right_matrix):
    return jnp.einsum("...ij,...jk->...ik", left_matrix, right_matrix, precision=lax.Precision.HIGHEST, preferred_element_type=jnp.float32)


def matmul_transposed(left_matrix, right_matrix):
    return jnp.einsum("...ij,...kj->...ik", left_matrix, right_matrix, precision=lax.Precision.HIGHEST, preferred_element_type=jnp.float32)


def complex_product(left_factor, right_factor):
    left_real, left_imag = left_factor[..., 0, :, :], left_factor[..., 1, :, :]
    right_real, right_imag = right_factor[..., 0, :, :], right_factor[..., 1, :, :]
    real_part = matmul_high(left_real, right_real) - matmul_high(left_imag, right_imag)
    imag_part = matmul_high(left_real, right_imag) + matmul_high(left_imag, right_real)
    return jnp.stack([real_part, imag_part], axis=-3)


def product_adjoint(left_factor, right_factor):
    left_real, left_imag = left_factor[..., 0, :, :], left_factor[..., 1, :, :]
    right_real, right_imag = right_factor[..., 0, :, :], right_factor[..., 1, :, :]
    real_part = matmul_transposed(left_real, right_real) + matmul_transposed(left_imag, right_imag)
    imag_part = matmul_transposed(left_imag, right_real) - matmul_transposed(left_real, right_imag)
    return jnp.stack([real_part, imag_part], axis=-3)


def masked_hopping(hopping_block, mask_block, tile_size):
    blocks = mask_block.shape[-1]
    expanded = jnp.broadcast_to(mask_block.astype(jnp.float32)[:, None, :, None], (blocks, tile_size, blocks, tile_size))
    return hopping_block * expanded.reshape(blocks * tile_size, blocks * tile_size)


def reference(retarded, lesser_prev, hopping, hop_mask, offsets, coupling, occupation):
    offsets_int = offsets.astype(jnp.int32)
    energies = lesser_prev.shape[1]
    results = []
    current = None
    for slab_index in range(SLABS):
        padded = jnp.pad(lesser_prev[slab_index], ((QMAX, QMAX), (0, 0), (0, 0), (0, 0)))
        self_energy = jnp.zeros(lesser_prev[slab_index].shape, jnp.float32)
        for mode_index in range(MODES):
            start_upper = (QMAX + offsets_int[mode_index]).astype(jnp.int32)
            start_lower = (QMAX - offsets_int[mode_index]).astype(jnp.int32)
            upper_piece = lax.dynamic_slice_in_dim(padded, start_upper, energies, 0)
            lower_piece = lax.dynamic_slice_in_dim(padded, start_lower, energies, 0)
            self_energy = self_energy + coupling[mode_index] * ((occupation[mode_index] + 1.0) * upper_piece + occupation[mode_index] * lower_piece)
        source = product_adjoint(complex_product(retarded[slab_index], self_energy), retarded[slab_index])
        if slab_index == 0:
            current = source
        else:
            coupled = matmul_high(retarded[slab_index], masked_hopping(hopping[slab_index], hop_mask[slab_index], TILE))
            current = source + product_adjoint(complex_product(coupled, current), coupled)
        results.append(current)
    return jnp.stack(results)
```

```python
import functools

import jax
import jax.numpy as jnp
from jax import lax
from jax.experimental import pallas as pl
from jax.experimental.pallas import tpu as pltpu
from jax.sharding import PartitionSpec as P

VMEM = pl.BlockSpec(memory_space=pltpu.VMEM)
SMEM = pl.BlockSpec(memory_space=pltpu.SMEM)
CHUNK_ROWS = 32
SMALL_VMEM = 8 * 1024 * 1024
LARGE_VMEM = 24 * 1024 * 1024


def combine_kernel(base, counts, weights_ref, *refs):
    inputs, outputs = refs[: len(counts)], refs[len(counts):]
    blocks = [(ref, index) for ref, count in zip(inputs, counts) for index in range(count)]
    targets = [(ref, index) for ref in outputs for index in range(ref.shape[0])]
    rows, columns = outputs[0].shape[1:]
    lanes = weights_ref.shape[2]
    for top in range(0, rows, CHUNK_ROWS):
        for left in range(0, columns, lanes):
            window = (slice(top, top + CHUNK_ROWS), slice(left, left + lanes))
            totals = [None] * len(targets)
            for column, (ref, index) in enumerate(blocks):
                value = ref[(index,) + window].reshape(CHUNK_ROWS // 8, 8, lanes)
                for row in range(len(targets)):
                    term = weights_ref[base + row * len(blocks) + column][None] * value
                    totals[row] = term if totals[row] is None else totals[row] + term
            for (ref, index), total in zip(targets, totals):
                ref[(index,) + window] = total.reshape(CHUNK_ROWS, lanes)


def combine(weights, base, inputs, output_count):
    counts = tuple(array.shape[0] for array in inputs)
    shape = jax.ShapeDtypeStruct(inputs[0].shape, jnp.float32)
    moved = sum(counts) + output_count * shape.shape[0]
    block_size = shape.shape[1] * shape.shape[2]
    result = pl.pallas_call(
        functools.partial(combine_kernel, base, counts),
        out_shape=[shape] * output_count,
        in_specs=[VMEM] * (1 + len(inputs)),
        out_specs=[VMEM] * output_count,
        compiler_params=pltpu.CompilerParams(vmem_limit_bytes=SMALL_VMEM),
        cost_estimate=pl.CostEstimate(
            flops=2 * block_size * sum(counts), bytes_accessed=4 * block_size * moved, transcendentals=0
        ),
    )(weights, *inputs)
    return result if output_count > 1 else result[0]


def weights_layout(per_device):
    sizes = [(2, 3), (2, 3), (1, 4), (1, 7), (1, 6), (1, 5)]
    bases = [0]
    for outputs, inputs in sizes:
        bases.append(bases[-1] + outputs * inputs * per_device**2)
    return bases


def weights_kernel(total_energies, per_device, offsets_ref, coupling_ref, occupation_ref, table_ref):
    modes = offsets_ref.shape[0]
    offsets = [offsets_ref[mode] for mode in range(modes)]
    lower = [coupling_ref[mode] * occupation_ref[mode] for mode in range(modes)]
    upper = [coupling_ref[mode] * (occupation_ref[mode] + 1.0) for mode in range(modes)]
    bases = weights_layout(per_device)

    me = lax.axis_index("energy")
    core, y, z = me % 2, (me // 2) % 2, me // 4
    chip = me // 2
    swapped = ((z % 2) == 0) == (y == 1)
    first_far_real = core == 1 - y
    away = 2 * y - 1
    beside, diagonal = chip - away, chip + away

    def energy(at_chip, at_core, index):
        return (2 * at_chip + at_core) * per_device + index

    def own(index):
        return energy(chip, core, index)

    def sibling(index):
        return energy(chip, 1 - core, index)

    def far1(index):
        return energy(chip + 2 * away, 1 - y, index)

    def far2(index):
        return energy(chip - 2 * away, y, index)

    def at(place):
        return lambda index: energy(place, core, index)

    def weight(targets, sources, condition=None):
        def entry(row, column):
            target, source = targets(row), sources(column)
            delta = source - target
            result = jnp.float32(0.0)
            for mode in range(modes):
                result = result + jnp.where(delta == offsets[mode], upper[mode], 0.0)
                result = result + jnp.where(delta == -offsets[mode], lower[mode], 0.0)
            inside = (source >= 0) & (source < total_energies)
            if condition is not None:
                inside = inside & condition
            return jnp.where(inside, result, 0.0)

        return entry

    def same(condition=None):
        def entry(row, column):
            if row != column:
                return jnp.float32(0.0)
            return jnp.float32(1.0) if condition is None else jnp.where(condition, 1.0, 0.0)

        return entry

    def choose(condition, one, other):
        return lambda row, column: jnp.where(condition, one(row, column), other(row, column))

    def none(row, column):
        return jnp.float32(0.0)

    def add(one, other):
        return lambda row, column: one(row, column) + other(row, column)

    real1, real2 = first_far_real, ~first_far_real
    here, there = swapped, ~swapped
    diagonal_at, beside_at = at(diagonal), at(beside)
    sum_row = [weight(diagonal_at, own), weight(diagonal_at, sibling), none]
    far1_row = [none, same(~real1), same(real1)]
    pass_row = [same(), none, none]
    far2_row = [none, same(~real2), same(real2)]
    tables = [
        [
            [choose(swapped, a, b) for a, b in zip(sum_row, far1_row)],
            [choose(swapped, b, a) for a, b in zip(sum_row, far1_row)],
        ],
        [
            [choose(swapped, a, b) for a, b in zip(far2_row, pass_row)],
            [choose(swapped, b, a) for a, b in zip(far2_row, pass_row)],
        ],
        [[weight(beside_at, own), weight(beside_at, sibling), same(there), same(here)]],
        [
            [
                weight(own, own),
                weight(own, sibling),
                same(),
                weight(own, far1, ~real1 & here),
                weight(own, far1, ~real1 & there),
                weight(own, far2, ~real2 & there),
                weight(own, far2, ~real2 & here),
            ]
        ],
        [
            [
                weight(sibling, own),
                weight(sibling, beside_at),
                weight(sibling, far1, real1 & here),
                weight(sibling, far1, real1 & there),
                add(weight(sibling, diagonal_at, here), weight(sibling, far2, real2 & there)),
                add(weight(sibling, diagonal_at, there), weight(sibling, far2, real2 & here)),
            ]
        ],
        [
            [
                weight(own, own),
                weight(own, beside_at),
                weight(own, diagonal_at, here),
                weight(own, diagonal_at, there),
                same(),
            ]
        ],
    ]
    for base, table in zip(bases, tables):
        place = base
        for row in table:
            for row_index in range(per_device):
                for entry in row:
                    for column_index in range(per_device):
                        value = entry(row_index, column_index)
                        table_ref[place] = jnp.full(table_ref.shape[1:], value, jnp.float32)
                        place += 1


def split(value):
    high = value.astype(jnp.bfloat16)
    low = (value - high.astype(jnp.float32)).astype(jnp.bfloat16)
    return high, low


def dot3(left, right, transposed=False):
    numbers = (((1,), (1 if transposed else 0,)), ((), ()))

    def one(a, b):
        return lax.dot_general(a, b, numbers, preferred_element_type=jnp.float32)

    return one(left[0], right[0]) + (one(left[0], right[1]) + one(left[1], right[0]))


def times(left, right):
    real = dot3(left[0], right[0]) - dot3(left[1], right[1])
    imag = dot3(left[0], right[1]) + dot3(left[1], right[0])
    return real, imag


def times_adjoint(left, right):
    real = dot3(left[0], right[0], True) + dot3(left[1], right[1], True)
    imag = dot3(left[1], right[0], True) - dot3(left[0], right[1], True)
    return real, imag


def split_pair(pair):
    return split(pair[0]), split(pair[1])


def bridge_kernel(tiles, mask_ref, hopping_ref, retarded_ref, behind_ref, coupled_ref, bridge_ref):
    size = hopping_ref.shape[0]
    tile = size // tiles
    row_tile = lax.broadcasted_iota(jnp.int32, (size, size), 0) // tile
    column_tile = lax.broadcasted_iota(jnp.int32, (size, size), 1) // tile
    mask = jnp.zeros((size, size), jnp.float32)
    for row in range(tiles):
        for column in range(tiles):
            here = (row_tile == row) & (column_tile == column)
            mask = jnp.where(here, mask_ref[row, column].astype(jnp.float32), mask)
    masked = split(hopping_ref[...] * mask)
    for energy in range(retarded_ref.shape[0]):
        coupled = tuple(dot3(split(retarded_ref[energy, part]), masked) for part in range(2))
        for part in range(2):
            coupled_ref[energy, part] = coupled[part]
        bridge = times(
            split_pair(coupled), split_pair((behind_ref[energy, 0], behind_ref[energy, 1]))
        )
        for part in range(2):
            bridge_ref[energy, part] = bridge[part]


def source_kernel(retarded_ref, real_ref, imag_ref, out_ref):
    for energy in range(retarded_ref.shape[0]):
        retarded = split_pair((retarded_ref[energy, 0], retarded_ref[energy, 1]))
        inner = times(retarded, split_pair((real_ref[energy], imag_ref[energy])))
        outer = times_adjoint(split_pair(inner), retarded)
        for part in range(2):
            out_ref[energy, part] = outer[part]


def imag_half_kernel(bridge_ref, imag_ref, out_ref):
    for energy in range(bridge_ref.shape[0]):
        imag = split(imag_ref[energy])
        out_ref[energy, 0] = -dot3(split(bridge_ref[energy, 1]), imag)
        out_ref[energy, 1] = dot3(split(bridge_ref[energy, 0]), imag)


def finish_kernel(flag_ref, bridge_ref, half_ref, real_ref, source_ref, out_ref):
    @pl.when(flag_ref[0] == 0)
    def _():
        out_ref[...] = source_ref[...]

    @pl.when(flag_ref[0] != 0)
    def _():
        for energy in range(bridge_ref.shape[0]):
            bridge = split_pair((bridge_ref[energy, 0], bridge_ref[energy, 1]))
            real = split(real_ref[energy])
            inner = tuple(half_ref[energy, part] + dot3(bridge[part], real) for part in range(2))
            outer = times_adjoint(split_pair(inner), bridge)
            for part in range(2):
                out_ref[energy, part] = source_ref[energy, part] + outer[part]


def advance_kernel(flag_ref, coupled_ref, incoming_ref, source_ref, current_ref, out_ref):
    @pl.when(flag_ref[0] == 0)
    def _():
        out_ref[...] = current_ref[...]

    @pl.when(flag_ref[0] != 0)
    def _():
        for energy in range(coupled_ref.shape[0]):
            coupled = split_pair((coupled_ref[energy, 0], coupled_ref[energy, 1]))
            inner = times(coupled, split_pair((incoming_ref[energy, 0], incoming_ref[energy, 1])))
            outer = times_adjoint(split_pair(inner), coupled)
            for part in range(2):
                out_ref[energy, part] = source_ref[energy, part] + outer[part]


def call(kernel, inputs, specs, outputs, products):
    size = outputs[0].shape[-1]
    return pl.pallas_call(
        kernel,
        out_shape=[jax.ShapeDtypeStruct(array.shape, jnp.float32) for array in outputs],
        in_specs=specs,
        out_specs=[VMEM] * len(outputs),
        compiler_params=pltpu.CompilerParams(vmem_limit_bytes=LARGE_VMEM),
        cost_estimate=pl.CostEstimate(
            flops=6 * products * size**3,
            bytes_accessed=4 * sum(array.size for array in list(inputs) + list(outputs)),
            transcendentals=0,
        ),
    )(*inputs)


def body(retarded, lesser_prev, hopping, hop_mask, offsets, coupling, occupation):
    devices = lax.axis_size("energy")
    slabs = lax.axis_size("slab")
    per_device = lesser_prev.shape[1]
    assert offsets.shape[0] == 3 and devices % 4 == 0
    bases = weights_layout(per_device)
    weights = pl.pallas_call(
        functools.partial(weights_kernel, per_device * devices, per_device),
        out_shape=jax.ShapeDtypeStruct((bases[-1], 8, 128), jnp.float32),
        in_specs=[SMEM] * 3,
        out_specs=VMEM,
        compiler_params=pltpu.CompilerParams(vmem_limit_bytes=SMALL_VMEM),
    )(offsets, coupling, occupation)

    def permute(value, pairs):
        return lax.ppermute(value, "energy", pairs)

    cores = [(i, i ^ 1) for i in range(devices)]
    across = [(i, i ^ 2) for i in range(devices)]
    first_lines = [(i, i ^ 4) for i in range(devices) if (i ^ 4) < devices]
    second_lines = []
    for i in range(devices):
        other = i + 4 if (i // 4) % 2 == 1 else i - 4
        if 0 <= other < devices:
            second_lines.append((i, other))
    ahead = [(s, (s + 1) % slabs) for s in range(slabs)]

    real, imag = lesser_prev[0, :, 0], lesser_prev[0, :, 1]
    blocks = retarded[0]
    imag_sibling = permute(imag, cores)
    real_beside = permute(real, across)
    behind = lax.ppermute(blocks, "slab", ahead)

    send1, send2 = combine(weights, bases[0], [imag, imag_sibling, real], 2)
    got1, got2 = permute(send1, first_lines), permute(send2, second_lines)
    send3, send4 = combine(weights, bases[1], [real_beside, imag_sibling, real], 2)
    got3, got4 = permute(send3, first_lines), permute(send4, second_lines)
    imag_beside = permute(
        combine(weights, bases[2], [imag, imag_sibling, got1, got2], 1), across
    )
    coupled, bridge = call(
        functools.partial(bridge_kernel, hop_mask.shape[-1]),
        [hop_mask[0], hopping[0], blocks, behind],
        [SMEM, VMEM, VMEM, VMEM],
        [blocks, blocks],
        12,
    )
    imag_beside, bridge = lax.optimization_barrier((imag_beside, bridge))
    self_imag = combine(
        weights, bases[3], [imag, imag_sibling, imag_beside, got1, got2, got3, got4], 1
    )
    self_imag_behind = lax.ppermute(self_imag, "slab", ahead)
    real_sibling = permute(
        combine(weights, bases[4], [real, real_beside, got1, got2, got3, got4], 1), cores
    )
    self_real = combine(weights, bases[5], [real, real_beside, got3, got4, real_sibling], 1)
    self_real_behind = lax.ppermute(self_real, "slab", ahead)

    (source,) = call(source_kernel, [blocks, self_real, self_imag], [VMEM] * 3, [blocks], 16)
    (half,) = call(imag_half_kernel, [bridge, self_imag_behind], [VMEM] * 2, [blocks], 4)
    position = lax.axis_index("slab")
    turn_flag = (position == 1).astype(jnp.int32).reshape(1)
    (lesser,) = call(
        finish_kernel,
        [turn_flag, bridge, half, self_real_behind, source],
        [SMEM] + [VMEM] * 4,
        [blocks],
        12,
    )
    for turn in range(2, slabs):
        incoming = lax.ppermute(lesser, "slab", ahead)
        (lesser,) = call(
            advance_kernel,
            [(position == turn).astype(jnp.int32).reshape(1), coupled, incoming, source, lesser],
            [SMEM] + [VMEM] * 4,
            [blocks],
            16,
        )
    return lesser[None]


def solution(mesh):
    return jax.shard_map(
        body,
        mesh=mesh,
        in_specs=(
            P("slab", "energy", None, None, None),
            P("slab", "energy", None, None, None),
            P("slab", None, None),
            P("slab", None, None),
            P(),
            P(),
            P(),
        ),
        out_specs=P("slab", "energy", None, None, None),
        check_vma=False,
    )
```

```python
import functools

import jax
import jax.numpy as jnp
from jax import lax
from jax.experimental import pallas as pl
from jax.experimental.pallas import tpu as pltpu
from jax.sharding import PartitionSpec as P

VMEM = pl.BlockSpec(memory_space=pltpu.VMEM)
SMEM = pl.BlockSpec(memory_space=pltpu.SMEM)
CHUNK_ROWS = 32
PIECES = 2
FIRST_PARTS, PARTS = 5, 8
SMALL_VMEM = 8 * 1024 * 1024
LARGE_VMEM = 24 * 1024 * 1024


def combine_kernel(base, counts, weights_ref, *refs):
    inputs, outputs = refs[: len(counts)], refs[len(counts):]
    blocks = [(ref, index) for ref, count in zip(inputs, counts) for index in range(count)]
    targets = [(ref, index) for ref in outputs for index in range(ref.shape[0])]
    rows, columns = outputs[0].shape[1:]
    lanes = weights_ref.shape[2]
    for top in range(0, rows, CHUNK_ROWS):
        for left in range(0, columns, lanes):
            window = (slice(top, top + CHUNK_ROWS), slice(left, left + lanes))
            totals = [None] * len(targets)
            for column, (ref, index) in enumerate(blocks):
                value = ref[(index,) + window].reshape(CHUNK_ROWS // 8, 8, lanes)
                for row in range(len(targets)):
                    term = weights_ref[base + row * len(blocks) + column][None] * value
                    totals[row] = term if totals[row] is None else totals[row] + term
            for (ref, index), total in zip(targets, totals):
                ref[(index,) + window] = total.reshape(CHUNK_ROWS, lanes)


def combine(weights, base, inputs, output_count):
    counts = tuple(array.shape[0] for array in inputs)
    shape = jax.ShapeDtypeStruct(inputs[0].shape, jnp.float32)
    moved = sum(counts) + output_count * shape.shape[0]
    block_size = shape.shape[1] * shape.shape[2]
    result = pl.pallas_call(
        functools.partial(combine_kernel, base, counts),
        out_shape=[shape] * output_count,
        in_specs=[VMEM] * (1 + len(inputs)),
        out_specs=[VMEM] * output_count,
        compiler_params=pltpu.CompilerParams(vmem_limit_bytes=SMALL_VMEM),
        cost_estimate=pl.CostEstimate(
            flops=2 * block_size * sum(counts), bytes_accessed=4 * block_size * moved, transcendentals=0
        ),
    )(weights, *inputs)
    return result if output_count > 1 else result[0]


def weights_layout(per_device):
    sizes = [(2, 3), (2, 3), (1, 4), (1, 7), (1, 6), (1, 5)]
    bases = [0]
    for outputs, inputs in sizes:
        bases.append(bases[-1] + outputs * inputs * per_device**2)
    return bases


def weights_kernel(total_energies, per_device, offsets_ref, coupling_ref, occupation_ref, table_ref):
    modes = offsets_ref.shape[0]
    offsets = [offsets_ref[mode] for mode in range(modes)]
    lower = [coupling_ref[mode] * occupation_ref[mode] for mode in range(modes)]
    upper = [coupling_ref[mode] * (occupation_ref[mode] + 1.0) for mode in range(modes)]
    bases = weights_layout(per_device)

    me = lax.axis_index("energy")
    core, y, z = me % 2, (me // 2) % 2, me // 4
    chip = me // 2
    swapped = ((z % 2) == 0) == (y == 1)
    first_far_real = core == 1 - y
    away = 2 * y - 1
    beside, diagonal = chip - away, chip + away

    def energy(at_chip, at_core, index):
        return (2 * at_chip + at_core) * per_device + index

    def own(index):
        return energy(chip, core, index)

    def sibling(index):
        return energy(chip, 1 - core, index)

    def far1(index):
        return energy(chip + 2 * away, 1 - y, index)

    def far2(index):
        return energy(chip - 2 * away, y, index)

    def at(place):
        return lambda index: energy(place, core, index)

    def weight(targets, sources, condition=None):
        def entry(row, column):
            target, source = targets(row), sources(column)
            delta = source - target
            result = jnp.float32(0.0)
            for mode in range(modes):
                result = result + jnp.where(delta == offsets[mode], upper[mode], 0.0)
                result = result + jnp.where(delta == -offsets[mode], lower[mode], 0.0)
            inside = (source >= 0) & (source < total_energies)
            if condition is not None:
                inside = inside & condition
            return jnp.where(inside, result, 0.0)

        return entry

    def same(condition=None):
        def entry(row, column):
            if row != column:
                return jnp.float32(0.0)
            return jnp.float32(1.0) if condition is None else jnp.where(condition, 1.0, 0.0)

        return entry

    def choose(condition, one, other):
        return lambda row, column: jnp.where(condition, one(row, column), other(row, column))

    def none(row, column):
        return jnp.float32(0.0)

    def add(one, other):
        return lambda row, column: one(row, column) + other(row, column)

    real1, real2 = first_far_real, ~first_far_real
    here, there = swapped, ~swapped
    diagonal_at, beside_at = at(diagonal), at(beside)
    sum_row = [weight(diagonal_at, own), weight(diagonal_at, sibling), none]
    far1_row = [none, same(~real1), same(real1)]
    pass_row = [same(), none, none]
    far2_row = [none, same(~real2), same(real2)]
    tables = [
        [
            [choose(swapped, a, b) for a, b in zip(sum_row, far1_row)],
            [choose(swapped, b, a) for a, b in zip(sum_row, far1_row)],
        ],
        [
            [choose(swapped, a, b) for a, b in zip(far2_row, pass_row)],
            [choose(swapped, b, a) for a, b in zip(far2_row, pass_row)],
        ],
        [[weight(beside_at, own), weight(beside_at, sibling), same(there), same(here)]],
        [
            [
                weight(own, own),
                weight(own, sibling),
                same(),
                weight(own, far1, ~real1 & here),
                weight(own, far1, ~real1 & there),
                weight(own, far2, ~real2 & there),
                weight(own, far2, ~real2 & here),
            ]
        ],
        [
            [
                weight(sibling, own),
                weight(sibling, beside_at),
                weight(sibling, far1, real1 & here),
                weight(sibling, far1, real1 & there),
                add(weight(sibling, diagonal_at, here), weight(sibling, far2, real2 & there)),
                add(weight(sibling, diagonal_at, there), weight(sibling, far2, real2 & here)),
            ]
        ],
        [
            [
                weight(own, own),
                weight(own, beside_at),
                weight(own, diagonal_at, here),
                weight(own, diagonal_at, there),
                same(),
            ]
        ],
    ]
    for base, table in zip(bases, tables):
        place = base
        for row in table:
            for row_index in range(per_device):
                for entry in row:
                    for column_index in range(per_device):
                        value = entry(row_index, column_index)
                        table_ref[place] = jnp.full(table_ref.shape[1:], value, jnp.float32)
                        place += 1


def split(value):
    high = value.astype(jnp.bfloat16)
    low = (value - high.astype(jnp.float32)).astype(jnp.bfloat16)
    return high, low


def dot3(left, right, transposed=False):
    numbers = (((1,), (1 if transposed else 0,)), ((), ()))

    def one(a, b):
        return lax.dot_general(a, b, numbers, preferred_element_type=jnp.float32)

    return one(left[0], right[0]) + (one(left[0], right[1]) + one(left[1], right[0]))


def times(left, right):
    real = dot3(left[0], right[0]) - dot3(left[1], right[1])
    imag = dot3(left[0], right[1]) + dot3(left[1], right[0])
    return real, imag


def times_adjoint(left, right):
    real = dot3(left[0], right[0], True) + dot3(left[1], right[1], True)
    imag = dot3(left[1], right[0], True) - dot3(left[0], right[1], True)
    return real, imag


def split_pair(pair):
    return split(pair[0]), split(pair[1])


def bridge_kernel(tiles, mask_ref, hopping_ref, retarded_ref, behind_ref, coupled_ref, bridge_ref):
    size = hopping_ref.shape[0]
    tile = size // tiles
    row_tile = lax.broadcasted_iota(jnp.int32, (size, size), 0) // tile
    column_tile = lax.broadcasted_iota(jnp.int32, (size, size), 1) // tile
    mask = jnp.zeros((size, size), jnp.float32)
    for row in range(tiles):
        for column in range(tiles):
            here = (row_tile == row) & (column_tile == column)
            mask = jnp.where(here, mask_ref[row, column].astype(jnp.float32), mask)
    masked = split(hopping_ref[...] * mask)
    for energy in range(retarded_ref.shape[0]):
        coupled = tuple(dot3(split(retarded_ref[energy, part]), masked) for part in range(2))
        for part in range(2):
            coupled_ref[energy, part] = coupled[part]
        bridge = times(
            split_pair(coupled), split_pair((behind_ref[energy, 0], behind_ref[energy, 1]))
        )
        for part in range(2):
            bridge_ref[energy, part] = bridge[part]


def row_windows(size):
    cut = size * FIRST_PARTS // PARTS
    return [slice(0, cut), slice(cut, size)]


def source_kernel(pieces, retarded_ref, *refs):
    real_refs, imag_refs, out_ref = refs[:pieces], refs[pieces : 2 * pieces], refs[-1]
    for energy in range(retarded_ref.shape[0]):
        retarded = split_pair((retarded_ref[energy, 0], retarded_ref[energy, 1]))
        real = jnp.concatenate([ref[energy] for ref in real_refs], axis=0)
        imag = jnp.concatenate([ref[energy] for ref in imag_refs], axis=0)
        inner = times(retarded, split_pair((real, imag)))
        outer = times_adjoint(split_pair(inner), retarded)
        for part in range(2):
            out_ref[energy, part] = outer[part]


def piece_kernel(window, bridge_ref, real_ref, imag_ref, out_ref):
    for energy in range(bridge_ref.shape[0]):
        bridge = split_pair((bridge_ref[energy, 0, :, window], bridge_ref[energy, 1, :, window]))
        inner = times(bridge, split_pair((real_ref[energy], imag_ref[energy])))
        for part in range(2):
            out_ref[energy, part] = inner[part]


def imag_half_kernel(window, bridge_ref, imag_ref, total_ref, out_ref):
    for energy in range(bridge_ref.shape[0]):
        imag = split(imag_ref[energy])
        real_share = dot3(split(bridge_ref[energy, 1, :, window]), imag)
        imag_share = dot3(split(bridge_ref[energy, 0, :, window]), imag)
        out_ref[energy, 0] = total_ref[energy, 0] - real_share
        out_ref[energy, 1] = total_ref[energy, 1] + imag_share


def finish_kernel(window, flag_ref, bridge_ref, half_ref, real_ref, source_ref, out_ref):
    @pl.when(flag_ref[0] == 0)
    def _():
        out_ref[...] = source_ref[...]

    @pl.when(flag_ref[0] != 0)
    def _():
        for energy in range(bridge_ref.shape[0]):
            bridge = split_pair((bridge_ref[energy, 0], bridge_ref[energy, 1]))
            real = split(real_ref[energy])
            left = [(high[:, window], low[:, window]) for high, low in bridge]
            inner = tuple(half_ref[energy, part] + dot3(left[part], real) for part in range(2))
            outer = times_adjoint(split_pair(inner), bridge)
            for part in range(2):
                out_ref[energy, part] = source_ref[energy, part] + outer[part]


def advance_kernel(flag_ref, coupled_ref, incoming_ref, source_ref, current_ref, out_ref):
    @pl.when(flag_ref[0] == 0)
    def _():
        out_ref[...] = current_ref[...]

    @pl.when(flag_ref[0] != 0)
    def _():
        for energy in range(coupled_ref.shape[0]):
            coupled = split_pair((coupled_ref[energy, 0], coupled_ref[energy, 1]))
            inner = times(coupled, split_pair((incoming_ref[energy, 0], incoming_ref[energy, 1])))
            outer = times_adjoint(split_pair(inner), coupled)
            for part in range(2):
                out_ref[energy, part] = source_ref[energy, part] + outer[part]


def call(kernel, inputs, specs, outputs, products):
    size = outputs[0].shape[-1]
    return pl.pallas_call(
        kernel,
        out_shape=[jax.ShapeDtypeStruct(array.shape, jnp.float32) for array in outputs],
        in_specs=specs,
        out_specs=[VMEM] * len(outputs),
        compiler_params=pltpu.CompilerParams(vmem_limit_bytes=LARGE_VMEM),
        cost_estimate=pl.CostEstimate(
            flops=6 * products * size**3,
            bytes_accessed=4 * sum(array.size for array in list(inputs) + list(outputs)),
            transcendentals=0,
        ),
    )(*inputs)


def after(value, *gates):
    return lax.optimization_barrier((value,) + gates)[0]


def body(retarded, lesser_prev, hopping, hop_mask, offsets, coupling, occupation):
    devices = lax.axis_size("energy")
    slabs = lax.axis_size("slab")
    per_device = lesser_prev.shape[1]
    assert offsets.shape[0] == 3 and devices % 4 == 0
    bases = weights_layout(per_device)
    weights = pl.pallas_call(
        functools.partial(weights_kernel, per_device * devices, per_device),
        out_shape=jax.ShapeDtypeStruct((bases[-1], 8, 128), jnp.float32),
        in_specs=[SMEM] * 3,
        out_specs=VMEM,
        compiler_params=pltpu.CompilerParams(vmem_limit_bytes=SMALL_VMEM),
    )(offsets, coupling, occupation)

    def permute(value, pairs):
        return lax.ppermute(value, "energy", pairs)

    cores = [(i, i ^ 1) for i in range(devices)]
    across = [(i, i ^ 2) for i in range(devices)]
    first_lines = [(i, i ^ 4) for i in range(devices) if (i ^ 4) < devices]
    second_lines = []
    for i in range(devices):
        other = i + 4 if (i // 4) % 2 == 1 else i - 4
        if 0 <= other < devices:
            second_lines.append((i, other))
    ahead = [(s, (s + 1) % slabs) for s in range(slabs)]

    blocks = retarded[0]
    size = blocks.shape[-1]
    windows = row_windows(size)
    behind = lax.ppermute(blocks, "slab", ahead)

    reals, imags, reals_behind, imags_behind = [], [], [], []
    gates = None
    for number, window in enumerate(windows):
        real, imag = lesser_prev[0, :, 0, window], lesser_prev[0, :, 1, window]
        real_sent, imag_own = real, imag
        imag_sibling = permute(imag, cores)
        if gates is not None:
            real_sent = after(real, gates[0])
            imag_own = after(imag, gates[1], gates[2])
        real_beside = permute(real_sent, across)
        send1, send2 = combine(weights, bases[0], [imag_own, imag_sibling, real], 2)
        got1, got2 = permute(send1, first_lines), permute(send2, second_lines)
        if gates is not None:
            real_beside = after(real_beside, gates[3])
        send3, send4 = combine(weights, bases[1], [real_beside, imag_sibling, real], 2)
        got3, got4 = permute(send3, first_lines), permute(send4, second_lines)
        if number == PIECES - 1:
            got1, behind = lax.optimization_barrier((got1, behind))
        if gates is not None:
            got1 = after(got1, imags_behind[-1])
        beside_sum = combine(weights, bases[2], [imag, imag_sibling, got1, got2], 1)
        imag_beside = permute(beside_sum, across)
        if gates is not None:
            pass
        self_imag = combine(
            weights, bases[3], [imag, imag_sibling, imag_beside, got1, got2, got3, got4], 1
        )
        real_late = real if gates is None else after(real, self_imag)
        sibling_sum = combine(weights, bases[4], [real_late, real_beside, got1, got2, got3, got4], 1)
        real_sibling = permute(sibling_sum, cores)
        if gates is not None:
            real_sibling = after(real_sibling, reals_behind[-1])
        self_real = combine(weights, bases[5], [real, real_beside, got3, got4, real_sibling], 1)
        gates = (imag_beside, self_imag, sibling_sum, self_real)
        imags.append(self_imag)
        reals.append(self_real)
        imags_behind.append(lax.ppermute(self_imag, "slab", ahead))
        reals_behind.append(lax.ppermute(self_real, "slab", ahead))

    behind, reals[-1] = lax.optimization_barrier((behind, reals[-1]))
    coupled, bridge = call(
        functools.partial(bridge_kernel, hop_mask.shape[-1]),
        [hop_mask[0], hopping[0], blocks, behind],
        [SMEM, VMEM, VMEM, VMEM],
        [blocks, blocks],
        12,
    )
    (source,) = call(
        functools.partial(source_kernel, PIECES),
        [blocks] + reals + imags,
        [VMEM] * (1 + 2 * PIECES),
        [blocks],
        16,
    )
    (total,) = call(
        functools.partial(piece_kernel, windows[0]),
        [bridge, reals_behind[0], imags_behind[0]],
        [VMEM] * 3,
        [blocks],
        8,
    )
    (half,) = call(
        functools.partial(imag_half_kernel, windows[-1]),
        [bridge, imags_behind[-1], after(total, source)],
        [VMEM] * 3,
        [blocks],
        4,
    )
    position = lax.axis_index("slab")
    turn_flag = (position == 1).astype(jnp.int32).reshape(1)
    (lesser,) = call(
        functools.partial(finish_kernel, windows[-1]),
        [turn_flag, bridge, half, reals_behind[-1], source],
        [SMEM] + [VMEM] * 4,
        [blocks],
        12,
    )
    for turn in range(2, slabs):
        incoming = lax.ppermute(lesser, "slab", ahead)
        (lesser,) = call(
            advance_kernel,
            [(position == turn).astype(jnp.int32).reshape(1), coupled, incoming, source, lesser],
            [SMEM] + [VMEM] * 4,
            [blocks],
            16,
        )
    return lesser[None]


def solution(mesh):
    return jax.shard_map(
        body,
        mesh=mesh,
        in_specs=(
            P("slab", "energy", None, None, None),
            P("slab", "energy", None, None, None),
            P("slab", None, None),
            P("slab", None, None),
            P(),
            P(),
            P(),
        ),
        out_specs=P("slab", "energy", None, None, None),
        check_vma=False,
    )
```

```python
import functools

import jax
import jax.numpy as jnp
from jax import lax
from jax.experimental import pallas as pl
from jax.experimental.pallas import tpu as pltpu
from jax.sharding import PartitionSpec as P

VMEM = pl.BlockSpec(memory_space=pltpu.VMEM)
SMEM = pl.BlockSpec(memory_space=pltpu.SMEM)
CHUNK_ROWS = 32
PIECES = 2
FIRST_PARTS, PARTS = 5, 8
SMALL_VMEM = 8 * 1024 * 1024
LARGE_VMEM = 24 * 1024 * 1024


def combine_kernel(base, counts, weights_ref, *refs):
    inputs, outputs = refs[: len(counts)], refs[len(counts):]
    blocks = [(ref, index) for ref, count in zip(inputs, counts) for index in range(count)]
    targets = [(ref, index) for ref in outputs for index in range(ref.shape[0])]
    rows, columns = outputs[0].shape[1:]
    lanes = weights_ref.shape[2]
    for top in range(0, rows, CHUNK_ROWS):
        for left in range(0, columns, lanes):
            window = (slice(top, top + CHUNK_ROWS), slice(left, left + lanes))
            totals = [None] * len(targets)
            for column, (ref, index) in enumerate(blocks):
                value = ref[(index,) + window].reshape(CHUNK_ROWS // 8, 8, lanes)
                for row in range(len(targets)):
                    term = weights_ref[base + row * len(blocks) + column][None] * value
                    totals[row] = term if totals[row] is None else totals[row] + term
            for (ref, index), total in zip(targets, totals):
                ref[(index,) + window] = total.reshape(CHUNK_ROWS, lanes)


def combine(weights, base, inputs, output_count):
    counts = tuple(array.shape[0] for array in inputs)
    shape = jax.ShapeDtypeStruct(inputs[0].shape, jnp.float32)
    moved = sum(counts) + output_count * shape.shape[0]
    block_size = shape.shape[1] * shape.shape[2]
    result = pl.pallas_call(
        functools.partial(combine_kernel, base, counts),
        out_shape=[shape] * output_count,
        in_specs=[VMEM] * (1 + len(inputs)),
        out_specs=[VMEM] * output_count,
        compiler_params=pltpu.CompilerParams(vmem_limit_bytes=SMALL_VMEM),
        cost_estimate=pl.CostEstimate(
            flops=2 * block_size * sum(counts), bytes_accessed=4 * block_size * moved, transcendentals=0
        ),
    )(weights, *inputs)
    return result if output_count > 1 else result[0]


def weights_layout(per_device):
    sizes = [(2, 3), (2, 3), (1, 4), (1, 7), (1, 6), (1, 5)]
    bases = [0]
    for outputs, inputs in sizes:
        bases.append(bases[-1] + outputs * inputs * per_device**2)
    return bases


def weights_kernel(total_energies, per_device, offsets_ref, coupling_ref, occupation_ref, table_ref):
    modes = offsets_ref.shape[0]
    offsets = [offsets_ref[mode] for mode in range(modes)]
    lower = [coupling_ref[mode] * occupation_ref[mode] for mode in range(modes)]
    upper = [coupling_ref[mode] * (occupation_ref[mode] + 1.0) for mode in range(modes)]
    bases = weights_layout(per_device)

    me = lax.axis_index("energy")
    core, y, z = me % 2, (me // 2) % 2, me // 4
    chip = me // 2
    swapped = ((z % 2) == 0) == (y == 1)
    first_far_real = core == 1 - y
    away = 2 * y - 1
    beside, diagonal = chip - away, chip + away

    def energy(at_chip, at_core, index):
        return (2 * at_chip + at_core) * per_device + index

    def own(index):
        return energy(chip, core, index)

    def sibling(index):
        return energy(chip, 1 - core, index)

    def far1(index):
        return energy(chip + 2 * away, 1 - y, index)

    def far2(index):
        return energy(chip - 2 * away, y, index)

    def at(place):
        return lambda index: energy(place, core, index)

    def weight(targets, sources, condition=None):
        def entry(row, column):
            target, source = targets(row), sources(column)
            delta = source - target
            result = jnp.float32(0.0)
            for mode in range(modes):
                result = result + jnp.where(delta == offsets[mode], upper[mode], 0.0)
                result = result + jnp.where(delta == -offsets[mode], lower[mode], 0.0)
            inside = (source >= 0) & (source < total_energies)
            if condition is not None:
                inside = inside & condition
            return jnp.where(inside, result, 0.0)

        return entry

    def same(condition=None):
        def entry(row, column):
            if row != column:
                return jnp.float32(0.0)
            return jnp.float32(1.0) if condition is None else jnp.where(condition, 1.0, 0.0)

        return entry

    def choose(condition, one, other):
        return lambda row, column: jnp.where(condition, one(row, column), other(row, column))

    def none(row, column):
        return jnp.float32(0.0)

    def add(one, other):
        return lambda row, column: one(row, column) + other(row, column)

    real1, real2 = first_far_real, ~first_far_real
    here, there = swapped, ~swapped
    diagonal_at, beside_at = at(diagonal), at(beside)
    sum_row = [weight(diagonal_at, own), weight(diagonal_at, sibling), none]
    far1_row = [none, same(~real1), same(real1)]
    pass_row = [same(), none, none]
    far2_row = [none, same(~real2), same(real2)]
    tables = [
        [
            [choose(swapped, a, b) for a, b in zip(sum_row, far1_row)],
            [choose(swapped, b, a) for a, b in zip(sum_row, far1_row)],
        ],
        [
            [choose(swapped, a, b) for a, b in zip(far2_row, pass_row)],
            [choose(swapped, b, a) for a, b in zip(far2_row, pass_row)],
        ],
        [[weight(beside_at, own), weight(beside_at, sibling), same(there), same(here)]],
        [
            [
                weight(own, own),
                weight(own, sibling),
                same(),
                weight(own, far1, ~real1 & here),
                weight(own, far1, ~real1 & there),
                weight(own, far2, ~real2 & there),
                weight(own, far2, ~real2 & here),
            ]
        ],
        [
            [
                weight(sibling, own),
                weight(sibling, beside_at),
                weight(sibling, far1, real1 & here),
                weight(sibling, far1, real1 & there),
                add(weight(sibling, diagonal_at, here), weight(sibling, far2, real2 & there)),
                add(weight(sibling, diagonal_at, there), weight(sibling, far2, real2 & here)),
            ]
        ],
        [
            [
                weight(own, own),
                weight(own, beside_at),
                weight(own, diagonal_at, here),
                weight(own, diagonal_at, there),
                same(),
            ]
        ],
    ]
    for base, table in zip(bases, tables):
        place = base
        for row in table:
            for row_index in range(per_device):
                for entry in row:
                    for column_index in range(per_device):
                        value = entry(row_index, column_index)
                        table_ref[place] = jnp.full(table_ref.shape[1:], value, jnp.float32)
                        place += 1


def split(value):
    high = value.astype(jnp.bfloat16)
    low = (value - high.astype(jnp.float32)).astype(jnp.bfloat16)
    return high, low


def dot3(left, right, transposed=False):
    numbers = (((1,), (1 if transposed else 0,)), ((), ()))

    def one(a, b):
        return lax.dot_general(a, b, numbers, preferred_element_type=jnp.float32)

    return one(left[0], right[0]) + (one(left[0], right[1]) + one(left[1], right[0]))


def times(left, right):
    real = dot3(left[0], right[0]) - dot3(left[1], right[1])
    imag = dot3(left[0], right[1]) + dot3(left[1], right[0])
    return real, imag


def times_adjoint(left, right):
    real = dot3(left[0], right[0], True) + dot3(left[1], right[1], True)
    imag = dot3(left[1], right[0], True) - dot3(left[0], right[1], True)
    return real, imag


def split_pair(pair):
    return split(pair[0]), split(pair[1])


def bridge_kernel(tiles, mask_ref, hopping_ref, retarded_ref, behind_ref, bridge_ref, *coupled_refs):
    size = hopping_ref.shape[0]
    tile = size // tiles
    column_tile = lax.broadcasted_iota(jnp.int32, (1, size), 1) // tile
    strips = []
    for row in range(tiles):
        strip = jnp.zeros((1, size), jnp.float32)
        for column in range(tiles):
            strip = jnp.where(column_tile == column, mask_ref[row, column].astype(jnp.float32), strip)
        strips.append(hopping_ref[row * tile : (row + 1) * tile, :] * strip)
    masked = split(jnp.concatenate(strips, axis=0))
    for energy in range(retarded_ref.shape[0]):
        coupled = tuple(dot3(split(retarded_ref[energy, part]), masked) for part in range(2))
        for coupled_ref in coupled_refs:
            for part in range(2):
                coupled_ref[energy, part] = coupled[part]
        bridge = times(
            split_pair(coupled), split_pair((behind_ref[energy, 0], behind_ref[energy, 1]))
        )
        for part in range(2):
            bridge_ref[energy, part] = bridge[part]


def row_windows(size):
    cut = size * FIRST_PARTS // PARTS
    return [slice(0, cut), slice(cut, size)]


def source_kernel(pieces, retarded_ref, *refs):
    real_refs, imag_refs, out_ref = refs[:pieces], refs[pieces : 2 * pieces], refs[-1]
    for energy in range(retarded_ref.shape[0]):
        retarded = split_pair((retarded_ref[energy, 0], retarded_ref[energy, 1]))
        real = jnp.concatenate([ref[energy] for ref in real_refs], axis=0)
        imag = jnp.concatenate([ref[energy] for ref in imag_refs], axis=0)
        inner = times(retarded, split_pair((real, imag)))
        outer = times_adjoint(split_pair(inner), retarded)
        for part in range(2):
            out_ref[energy, part] = outer[part]


def piece_kernel(window, bridge_ref, real_ref, imag_ref, out_ref):
    for energy in range(bridge_ref.shape[0]):
        bridge = split_pair((bridge_ref[energy, 0, :, window], bridge_ref[energy, 1, :, window]))
        inner = times(bridge, split_pair((real_ref[energy], imag_ref[energy])))
        for part in range(2):
            out_ref[energy, part] = inner[part]


def imag_half_kernel(window, bridge_ref, imag_ref, total_ref, out_ref):
    for energy in range(bridge_ref.shape[0]):
        imag = split(imag_ref[energy])
        real_share = dot3(split(bridge_ref[energy, 1, :, window]), imag)
        imag_share = dot3(split(bridge_ref[energy, 0, :, window]), imag)
        out_ref[energy, 0] = total_ref[energy, 0] - real_share
        out_ref[energy, 1] = total_ref[energy, 1] + imag_share


def finish_kernel(window, flag_ref, bridge_ref, half_ref, real_ref, source_ref, out_ref):
    @pl.when(flag_ref[0] == 0)
    def _():
        out_ref[...] = source_ref[...]

    @pl.when(flag_ref[0] != 0)
    def _():
        for energy in range(bridge_ref.shape[0]):
            bridge = split_pair((bridge_ref[energy, 0], bridge_ref[energy, 1]))
            real = split(real_ref[energy])
            left = [(high[:, window], low[:, window]) for high, low in bridge]
            inner = tuple(half_ref[energy, part] + dot3(left[part], real) for part in range(2))
            outer = times_adjoint(split_pair(inner), bridge)
            for part in range(2):
                out_ref[energy, part] = source_ref[energy, part] + outer[part]


def advance_kernel(flag_ref, coupled_ref, incoming_ref, source_ref, current_ref, out_ref):
    @pl.when(flag_ref[0] == 0)
    def _():
        out_ref[...] = current_ref[...]

    @pl.when(flag_ref[0] != 0)
    def _():
        for energy in range(coupled_ref.shape[0]):
            coupled = split_pair((coupled_ref[energy, 0], coupled_ref[energy, 1]))
            inner = times(coupled, split_pair((incoming_ref[energy, 0], incoming_ref[energy, 1])))
            outer = times_adjoint(split_pair(inner), coupled)
            for part in range(2):
                out_ref[energy, part] = source_ref[energy, part] + outer[part]


def call(kernel, inputs, specs, outputs, products):
    size = outputs[0].shape[-1]
    return pl.pallas_call(
        kernel,
        out_shape=[jax.ShapeDtypeStruct(array.shape, jnp.float32) for array in outputs],
        in_specs=specs,
        out_specs=[VMEM] * len(outputs),
        compiler_params=pltpu.CompilerParams(vmem_limit_bytes=LARGE_VMEM),
        cost_estimate=pl.CostEstimate(
            flops=6 * products * size**3,
            bytes_accessed=4 * sum(array.size for array in list(inputs) + list(outputs)),
            transcendentals=0,
        ),
    )(*inputs)


def after(value, *gates):
    return lax.optimization_barrier((value,) + gates)[0]


def body(retarded, lesser_prev, hopping, hop_mask, offsets, coupling, occupation):
    devices = lax.axis_size("energy")
    slabs = lax.axis_size("slab")
    per_device = lesser_prev.shape[1]
    assert offsets.shape[0] == 3 and devices % 4 == 0
    bases = weights_layout(per_device)
    weights = pl.pallas_call(
        functools.partial(weights_kernel, per_device * devices, per_device),
        out_shape=jax.ShapeDtypeStruct((bases[-1], 8, 128), jnp.float32),
        in_specs=[SMEM] * 3,
        out_specs=VMEM,
        compiler_params=pltpu.CompilerParams(vmem_limit_bytes=SMALL_VMEM),
    )(offsets, coupling, occupation)

    def permute(value, pairs, name):
        with jax.named_scope(name):
            return lax.ppermute(value, "energy", pairs)

    def to_next_slab(value, name):
        with jax.named_scope(name):
            return lax.ppermute(value, "slab", ahead)

    cores = [(i, i ^ 1) for i in range(devices)]
    across = [(i, i ^ 2) for i in range(devices)]
    first_lines = [(i, i ^ 4) for i in range(devices) if (i ^ 4) < devices]
    second_lines = []
    for i in range(devices):
        other = i + 4 if (i // 4) % 2 == 1 else i - 4
        if 0 <= other < devices:
            second_lines.append((i, other))
    ahead = [(s, (s + 1) % slabs) for s in range(slabs)]

    blocks = retarded[0]
    size = blocks.shape[-1]
    windows = row_windows(size)
    behind = to_next_slab(blocks, "slab_retarded")

    reals, imags, reals_behind, imags_behind = [], [], [], []
    gates = None
    for number, window in enumerate(windows):
        real, imag = lesser_prev[0, :, 0, window], lesser_prev[0, :, 1, window]
        real_sent, imag_own = real, imag
        imag_sibling = permute(imag, cores, f"imag_cores_{number}")
        if gates is not None:
            real_sent = after(real, gates[0])
            imag_own = after(imag, gates[1])
        real_beside = permute(real_sent, across, f"real_across_{number}")
        send1, send2 = combine(weights, bases[0], [imag_own, imag_sibling, real], 2)
        got1 = permute(send1, first_lines, f"lines1a_{number}")
        got2 = permute(send2, second_lines, f"lines1b_{number}")
        if gates is not None:
            real_beside = after(real_beside, gates[2])
        send3, send4 = combine(weights, bases[1], [real_beside, imag_sibling, real], 2)
        got4 = permute(send4, second_lines, f"lines2b_{number}")
        got3 = permute(send3, first_lines, f"lines2a_{number}")
        if number == PIECES - 1:
            got1, behind = lax.optimization_barrier((got1, behind))
        if gates is not None:
            got1 = after(got1, imags_behind[-1])
        beside_sum = combine(weights, bases[2], [imag, imag_sibling, got1, got2], 1)
        imag_beside = permute(beside_sum, across, f"imag_across_{number}")
        self_imag = combine(
            weights, bases[3], [imag, imag_sibling, imag_beside, got1, got2, got3, got4], 1
        )
        real_late = real if gates is None else after(real, self_imag)
        sibling_sum = combine(weights, bases[4], [real_late, real_beside, got1, got2, got3, got4], 1)
        real_sibling = permute(sibling_sum, cores, f"real_cores_{number}")
        if gates is not None:
            real_sibling = after(real_sibling, reals_behind[-1])
        self_real = combine(weights, bases[5], [real, real_beside, got3, got4, real_sibling], 1)
        gates = (imag_beside, self_imag, self_real)
        imags.append(self_imag)
        reals.append(self_real)
        imags_behind.append(to_next_slab(self_imag, f"slab_imag_{number}"))
        reals_behind.append(to_next_slab(self_real, f"slab_real_{number}"))

    (source,) = call(
        functools.partial(source_kernel, PIECES),
        [blocks] + reals + imags,
        [VMEM] * (1 + 2 * PIECES),
        [blocks],
        16,
    )
    bridge, *coupled = call(
        functools.partial(bridge_kernel, hop_mask.shape[-1]),
        [hop_mask[0], hopping[0], blocks, after(behind, source)],
        [SMEM, VMEM, VMEM, VMEM],
        [blocks] * (2 if slabs > 2 else 1),
        12,
    )
    (total,) = call(
        functools.partial(piece_kernel, windows[0]),
        [bridge, reals_behind[0], imags_behind[0]],
        [VMEM] * 3,
        [blocks],
        8,
    )
    (half,) = call(
        functools.partial(imag_half_kernel, windows[-1]),
        [bridge, imags_behind[-1], total],
        [VMEM] * 3,
        [blocks],
        4,
    )
    position = lax.axis_index("slab")
    turn_flag = (position == 1).astype(jnp.int32).reshape(1)
    (lesser,) = call(
        functools.partial(finish_kernel, windows[-1]),
        [turn_flag, bridge, half, reals_behind[-1], source],
        [SMEM] + [VMEM] * 4,
        [blocks],
        12,
    )
    for turn in range(2, slabs):
        incoming = lax.ppermute(lesser, "slab", ahead)
        (lesser,) = call(
            advance_kernel,
            [(position == turn).astype(jnp.int32).reshape(1), coupled[0], incoming, source, lesser],
            [SMEM] + [VMEM] * 4,
            [blocks],
            16,
        )
    return lesser[None]


def solution(mesh):
    return jax.shard_map(
        body,
        mesh=mesh,
        in_specs=(
            P("slab", "energy", None, None, None),
            P("slab", "energy", None, None, None),
            P("slab", None, None),
            P("slab", None, None),
            P(),
            P(),
            P(),
        ),
        out_specs=P("slab", "energy", None, None, None),
        check_vma=False,
    )
```

```python
import functools

import jax
import jax.numpy as jnp
from jax import lax
from jax.experimental import pallas as pl
from jax.experimental.pallas import tpu as pltpu
from jax.sharding import PartitionSpec as P

VMEM = pl.BlockSpec(memory_space=pltpu.VMEM)
SMEM = pl.BlockSpec(memory_space=pltpu.SMEM)
CHUNK_ROWS = 32
PIECES = 2
FIRST_PARTS, PARTS = 5, 8
SMALL_VMEM = 8 * 1024 * 1024
LARGE_VMEM = 24 * 1024 * 1024


def combine_kernel(base, counts, weights_ref, *refs):
    inputs, outputs = refs[: len(counts)], refs[len(counts):]
    blocks = [(ref, index) for ref, count in zip(inputs, counts) for index in range(count)]
    targets = [(ref, index) for ref in outputs for index in range(ref.shape[0])]
    rows, columns = outputs[0].shape[1:]
    lanes = weights_ref.shape[2]
    for top in range(0, rows, CHUNK_ROWS):
        for left in range(0, columns, lanes):
            window = (slice(top, top + CHUNK_ROWS), slice(left, left + lanes))
            totals = [None] * len(targets)
            for column, (ref, index) in enumerate(blocks):
                value = ref[(index,) + window].reshape(CHUNK_ROWS // 8, 8, lanes)
                for row in range(len(targets)):
                    term = weights_ref[base + row * len(blocks) + column][None] * value
                    totals[row] = term if totals[row] is None else totals[row] + term
            for (ref, index), total in zip(targets, totals):
                ref[(index,) + window] = total.reshape(CHUNK_ROWS, lanes)


def combine(weights, base, inputs, output_count):
    counts = tuple(array.shape[0] for array in inputs)
    shape = jax.ShapeDtypeStruct(inputs[0].shape, jnp.float32)
    moved = sum(counts) + output_count * shape.shape[0]
    block_size = shape.shape[1] * shape.shape[2]
    result = pl.pallas_call(
        functools.partial(combine_kernel, base, counts),
        out_shape=[shape] * output_count,
        in_specs=[VMEM] * (1 + len(inputs)),
        out_specs=[VMEM] * output_count,
        compiler_params=pltpu.CompilerParams(vmem_limit_bytes=SMALL_VMEM),
        cost_estimate=pl.CostEstimate(
            flops=2 * block_size * sum(counts), bytes_accessed=4 * block_size * moved, transcendentals=0
        ),
    )(weights, *inputs)
    return result if output_count > 1 else result[0]


def weights_layout(per_device):
    sizes = [(2, 3), (2, 3), (1, 4), (1, 7), (1, 6), (1, 5)]
    bases = [0]
    for outputs, inputs in sizes:
        bases.append(bases[-1] + outputs * inputs * per_device**2)
    return bases


def weights_kernel(total_energies, per_device, offsets_ref, coupling_ref, occupation_ref, table_ref):
    modes = offsets_ref.shape[0]
    offsets = [offsets_ref[mode] for mode in range(modes)]
    lower = [coupling_ref[mode] * occupation_ref[mode] for mode in range(modes)]
    upper = [coupling_ref[mode] * (occupation_ref[mode] + 1.0) for mode in range(modes)]
    bases = weights_layout(per_device)

    me = lax.axis_index("energy")
    core, y, z = me % 2, (me // 2) % 2, me // 4
    chip = me // 2
    swapped = ((z % 2) == 0) == (y == 1)
    first_far_real = core == 1 - y
    away = 2 * y - 1
    beside, diagonal = chip - away, chip + away

    def energy(at_chip, at_core, index):
        return (2 * at_chip + at_core) * per_device + index

    def own(index):
        return energy(chip, core, index)

    def sibling(index):
        return energy(chip, 1 - core, index)

    def far1(index):
        return energy(chip + 2 * away, 1 - y, index)

    def far2(index):
        return energy(chip - 2 * away, y, index)

    def at(place):
        return lambda index: energy(place, core, index)

    def weight(targets, sources, condition=None):
        def entry(row, column):
            target, source = targets(row), sources(column)
            delta = source - target
            result = jnp.float32(0.0)
            for mode in range(modes):
                result = result + jnp.where(delta == offsets[mode], upper[mode], 0.0)
                result = result + jnp.where(delta == -offsets[mode], lower[mode], 0.0)
            inside = (source >= 0) & (source < total_energies)
            if condition is not None:
                inside = inside & condition
            return jnp.where(inside, result, 0.0)

        return entry

    def same(condition=None):
        def entry(row, column):
            if row != column:
                return jnp.float32(0.0)
            return jnp.float32(1.0) if condition is None else jnp.where(condition, 1.0, 0.0)

        return entry

    def choose(condition, one, other):
        return lambda row, column: jnp.where(condition, one(row, column), other(row, column))

    def none(row, column):
        return jnp.float32(0.0)

    def add(one, other):
        return lambda row, column: one(row, column) + other(row, column)

    real1, real2 = first_far_real, ~first_far_real
    here, there = swapped, ~swapped
    diagonal_at, beside_at = at(diagonal), at(beside)
    sum_row = [weight(diagonal_at, own), weight(diagonal_at, sibling), none]
    far1_row = [none, same(~real1), same(real1)]
    pass_row = [same(), none, none]
    far2_row = [none, same(~real2), same(real2)]
    tables = [
        [
            [choose(swapped, a, b) for a, b in zip(sum_row, far1_row)],
            [choose(swapped, b, a) for a, b in zip(sum_row, far1_row)],
        ],
        [
            [choose(swapped, a, b) for a, b in zip(far2_row, pass_row)],
            [choose(swapped, b, a) for a, b in zip(far2_row, pass_row)],
        ],
        [[weight(beside_at, own), weight(beside_at, sibling), same(there), same(here)]],
        [
            [
                weight(own, own),
                weight(own, sibling),
                same(),
                weight(own, far1, ~real1 & here),
                weight(own, far1, ~real1 & there),
                weight(own, far2, ~real2 & there),
                weight(own, far2, ~real2 & here),
            ]
        ],
        [
            [
                weight(sibling, own),
                weight(sibling, beside_at),
                weight(sibling, far1, real1 & here),
                weight(sibling, far1, real1 & there),
                add(weight(sibling, diagonal_at, here), weight(sibling, far2, real2 & there)),
                add(weight(sibling, diagonal_at, there), weight(sibling, far2, real2 & here)),
            ]
        ],
        [
            [
                weight(own, own),
                weight(own, beside_at),
                weight(own, diagonal_at, here),
                weight(own, diagonal_at, there),
                same(),
            ]
        ],
    ]
    for base, table in zip(bases, tables):
        place = base
        for row in table:
            for row_index in range(per_device):
                for entry in row:
                    for column_index in range(per_device):
                        value = entry(row_index, column_index)
                        table_ref[place] = jnp.full(table_ref.shape[1:], value, jnp.float32)
                        place += 1


def split(value):
    high = value.astype(jnp.bfloat16)
    low = (value - high.astype(jnp.float32)).astype(jnp.bfloat16)
    return high, low


def dot3(left, right, transposed=False):
    numbers = (((1,), (1 if transposed else 0,)), ((), ()))

    def one(a, b):
        return lax.dot_general(a, b, numbers, preferred_element_type=jnp.float32)

    return one(left[0], right[0]) + (one(left[0], right[1]) + one(left[1], right[0]))


def times(left, right):
    real = dot3(left[0], right[0]) - dot3(left[1], right[1])
    imag = dot3(left[0], right[1]) + dot3(left[1], right[0])
    return real, imag


def times_adjoint(left, right):
    real = dot3(left[0], right[0], True) + dot3(left[1], right[1], True)
    imag = dot3(left[1], right[0], True) - dot3(left[0], right[1], True)
    return real, imag


def split_pair(pair):
    return split(pair[0]), split(pair[1])


def bridge_kernel(tiles, mask_ref, hopping_ref, retarded_ref, behind_ref, bridge_ref, *coupled_refs):
    size = hopping_ref.shape[0]
    tile = size // tiles
    column_tile = lax.broadcasted_iota(jnp.int32, (1, size), 1) // tile
    strips = []
    for row in range(tiles):
        strip = jnp.zeros((1, size), jnp.float32)
        for column in range(tiles):
            strip = jnp.where(column_tile == column, mask_ref[row, column].astype(jnp.float32), strip)
        strips.append(hopping_ref[row * tile : (row + 1) * tile, :] * strip)
    masked = split(jnp.concatenate(strips, axis=0))
    for energy in range(retarded_ref.shape[0]):
        coupled = tuple(dot3(split(retarded_ref[energy, part]), masked) for part in range(2))
        for coupled_ref in coupled_refs:
            for part in range(2):
                coupled_ref[energy, part] = coupled[part]
        bridge = times(
            split_pair(coupled), split_pair((behind_ref[energy, 0], behind_ref[energy, 1]))
        )
        for part in range(2):
            bridge_ref[energy, part] = bridge[part]


def row_windows(size):
    cut = size * FIRST_PARTS // PARTS
    return [slice(0, cut), slice(cut, size)]


def source_kernel(pieces, retarded_ref, *refs):
    real_refs, imag_refs, out_ref = refs[:pieces], refs[pieces : 2 * pieces], refs[-1]
    for energy in range(retarded_ref.shape[0]):
        retarded = split_pair((retarded_ref[energy, 0], retarded_ref[energy, 1]))
        real = jnp.concatenate([ref[energy] for ref in real_refs], axis=0)
        imag = jnp.concatenate([ref[energy] for ref in imag_refs], axis=0)
        inner = times(retarded, split_pair((real, imag)))
        outer = times_adjoint(split_pair(inner), retarded)
        for part in range(2):
            out_ref[energy, part] = outer[part]


def piece_kernel(window, bridge_ref, real_ref, imag_ref, out_ref):
    for energy in range(bridge_ref.shape[0]):
        bridge = split_pair((bridge_ref[energy, 0, :, window], bridge_ref[energy, 1, :, window]))
        inner = times(bridge, split_pair((real_ref[energy], imag_ref[energy])))
        for part in range(2):
            out_ref[energy, part] = inner[part]


def imag_half_kernel(window, bridge_ref, imag_ref, total_ref, out_ref):
    for energy in range(bridge_ref.shape[0]):
        imag = split(imag_ref[energy])
        real_share = dot3(split(bridge_ref[energy, 1, :, window]), imag)
        imag_share = dot3(split(bridge_ref[energy, 0, :, window]), imag)
        out_ref[energy, 0] = total_ref[energy, 0] - real_share
        out_ref[energy, 1] = total_ref[energy, 1] + imag_share


def finish_kernel(window, flag_ref, bridge_ref, half_ref, real_ref, source_ref, out_ref):
    @pl.when(flag_ref[0] == 0)
    def _():
        out_ref[...] = source_ref[...]

    @pl.when(flag_ref[0] != 0)
    def _():
        for energy in range(bridge_ref.shape[0]):
            bridge = split_pair((bridge_ref[energy, 0], bridge_ref[energy, 1]))
            real = split(real_ref[energy])
            left = [(high[:, window], low[:, window]) for high, low in bridge]
            inner = tuple(half_ref[energy, part] + dot3(left[part], real) for part in range(2))
            outer = times_adjoint(split_pair(inner), bridge)
            for part in range(2):
                out_ref[energy, part] = source_ref[energy, part] + outer[part]


def advance_kernel(flag_ref, coupled_ref, incoming_ref, source_ref, current_ref, out_ref):
    @pl.when(flag_ref[0] == 0)
    def _():
        out_ref[...] = current_ref[...]

    @pl.when(flag_ref[0] != 0)
    def _():
        for energy in range(coupled_ref.shape[0]):
            coupled = split_pair((coupled_ref[energy, 0], coupled_ref[energy, 1]))
            inner = times(coupled, split_pair((incoming_ref[energy, 0], incoming_ref[energy, 1])))
            outer = times_adjoint(split_pair(inner), coupled)
            for part in range(2):
                out_ref[energy, part] = source_ref[energy, part] + outer[part]


def call(kernel, inputs, specs, outputs, products):
    size = outputs[0].shape[-1]
    return pl.pallas_call(
        kernel,
        out_shape=[jax.ShapeDtypeStruct(array.shape, jnp.float32) for array in outputs],
        in_specs=specs,
        out_specs=[VMEM] * len(outputs),
        compiler_params=pltpu.CompilerParams(vmem_limit_bytes=LARGE_VMEM),
        cost_estimate=pl.CostEstimate(
            flops=6 * products * size**3,
            bytes_accessed=4 * sum(array.size for array in list(inputs) + list(outputs)),
            transcendentals=0,
        ),
    )(*inputs)


def after(value, *gates):
    return lax.optimization_barrier((value,) + gates)[0]


def body(retarded, lesser_prev, hopping, hop_mask, offsets, coupling, occupation):
    devices = lax.axis_size("energy")
    slabs = lax.axis_size("slab")
    per_device = lesser_prev.shape[1]
    assert offsets.shape[0] == 3 and devices % 4 == 0
    bases = weights_layout(per_device)
    weights = pl.pallas_call(
        functools.partial(weights_kernel, per_device * devices, per_device),
        out_shape=jax.ShapeDtypeStruct((bases[-1], 8, 128), jnp.float32),
        in_specs=[SMEM] * 3,
        out_specs=VMEM,
        compiler_params=pltpu.CompilerParams(vmem_limit_bytes=SMALL_VMEM),
    )(offsets, coupling, occupation)

    def permute(value, pairs, name):
        with jax.named_scope(name):
            return lax.ppermute(value, "energy", pairs)

    def to_next_slab(value, name):
        with jax.named_scope(name):
            return lax.ppermute(value, "slab", ahead)

    cores = [(i, i ^ 1) for i in range(devices)]
    across = [(i, i ^ 2) for i in range(devices)]
    first_lines = [(i, i ^ 4) for i in range(devices) if (i ^ 4) < devices]
    second_lines = []
    for i in range(devices):
        other = i + 4 if (i // 4) % 2 == 1 else i - 4
        if 0 <= other < devices:
            second_lines.append((i, other))
    ahead = [(s, (s + 1) % slabs) for s in range(slabs)]

    blocks = retarded[0]
    size = blocks.shape[-1]
    windows = row_windows(size)
    behind = to_next_slab(blocks, "slab_retarded")

    reals, imags, reals_behind, imags_behind = [], [], [], []
    gates = None
    for number, window in enumerate(windows):
        real, imag = lesser_prev[0, :, 0, window], lesser_prev[0, :, 1, window]
        real_sent, imag_own = real, imag
        imag_sibling = permute(imag, cores, f"imag_cores_{number}")
        if gates is not None:
            real_sent = after(real, gates[0])
            imag_own = after(imag, gates[1])
        real_beside = permute(real_sent, across, f"real_across_{number}")
        send1, send2 = combine(weights, bases[0], [imag_own, imag_sibling, real], 2)
        got1 = permute(send1, first_lines, f"lines1a_{number}")
        got2 = permute(send2, second_lines, f"lines1b_{number}")
        if gates is not None:
            real_beside = after(real_beside, gates[2])
        send3, send4 = combine(weights, bases[1], [real_beside, imag_sibling, real], 2)
        got4 = permute(send4, second_lines, f"lines2b_{number}")
        got3 = permute(send3, first_lines, f"lines2a_{number}")
        if number == PIECES - 1:
            got1, behind = lax.optimization_barrier((got1, behind))
        if gates is not None:
            got1 = after(got1, imags_behind[-1])
        beside_sum = combine(weights, bases[2], [imag, imag_sibling, got1, got2], 1)
        imag_beside = permute(beside_sum, across, f"imag_across_{number}")
        self_imag = combine(
            weights, bases[3], [imag, imag_sibling, imag_beside, got1, got2, got3, got4], 1
        )
        real_late = real if gates is None else after(real, self_imag)
        sibling_sum = combine(weights, bases[4], [real_late, real_beside, got1, got2, got3, got4], 1)
        real_sibling = permute(sibling_sum, cores, f"real_cores_{number}")
        if gates is not None:
            real_sibling = after(real_sibling, reals_behind[-1])
        self_real = combine(weights, bases[5], [real, real_beside, got3, got4, real_sibling], 1)
        gates = (real_beside, self_imag, self_real)
        imags.append(self_imag)
        reals.append(self_real)
        imags_behind.append(to_next_slab(self_imag, f"slab_imag_{number}"))
        reals_behind.append(to_next_slab(self_real, f"slab_real_{number}"))

    (source,) = call(
        functools.partial(source_kernel, PIECES),
        [blocks] + reals + imags,
        [VMEM] * (1 + 2 * PIECES),
        [blocks],
        16,
    )
    bridge, *coupled = call(
        functools.partial(bridge_kernel, hop_mask.shape[-1]),
        [hop_mask[0], hopping[0], blocks, after(behind, source)],
        [SMEM, VMEM, VMEM, VMEM],
        [blocks] * (2 if slabs > 2 else 1),
        12,
    )
    (total,) = call(
        functools.partial(piece_kernel, windows[0]),
        [bridge, reals_behind[0], imags_behind[0]],
        [VMEM] * 3,
        [blocks],
        8,
    )
    (half,) = call(
        functools.partial(imag_half_kernel, windows[-1]),
        [bridge, imags_behind[-1], total],
        [VMEM] * 3,
        [blocks],
        4,
    )
    position = lax.axis_index("slab")
    turn_flag = (position == 1).astype(jnp.int32).reshape(1)
    (lesser,) = call(
        functools.partial(finish_kernel, windows[-1]),
        [turn_flag, bridge, half, reals_behind[-1], source],
        [SMEM] + [VMEM] * 4,
        [blocks],
        12,
    )
    for turn in range(2, slabs):
        incoming = lax.ppermute(lesser, "slab", ahead)
        (lesser,) = call(
            advance_kernel,
            [(position == turn).astype(jnp.int32).reshape(1), coupled[0], incoming, source, lesser],
            [SMEM] + [VMEM] * 4,
            [blocks],
            16,
        )
    return lesser[None]


def solution(mesh):
    return jax.shard_map(
        body,
        mesh=mesh,
        in_specs=(
            P("slab", "energy", None, None, None),
            P("slab", "energy", None, None, None),
            P("slab", None, None),
            P("slab", None, None),
            P(),
            P(),
            P(),
        ),
        out_specs=P("slab", "energy", None, None, None),
        check_vma=False,
    )
```

```python
import functools

import jax
import jax.numpy as jnp
from jax import lax
from jax.experimental import pallas as pl
from jax.experimental.pallas import tpu as pltpu
from jax.sharding import PartitionSpec as P

VMEM = pl.BlockSpec(memory_space=pltpu.VMEM)
SMEM = pl.BlockSpec(memory_space=pltpu.SMEM)
CHUNK_ROWS = 32
PIECES = 2
FIRST_PARTS, PARTS = 5, 8
SMALL_VMEM = 8 * 1024 * 1024
LARGE_VMEM = 24 * 1024 * 1024


def combine_kernel(base, counts, weights_ref, *refs):
    inputs, outputs = refs[: len(counts)], refs[len(counts):]
    blocks = [(ref, index) for ref, count in zip(inputs, counts) for index in range(count)]
    targets = [(ref, index) for ref in outputs for index in range(ref.shape[0])]
    rows, columns = outputs[0].shape[1:]
    lanes = weights_ref.shape[2]
    for top in range(0, rows, CHUNK_ROWS):
        for left in range(0, columns, lanes):
            window = (slice(top, top + CHUNK_ROWS), slice(left, left + lanes))
            totals = [None] * len(targets)
            for column, (ref, index) in enumerate(blocks):
                value = ref[(index,) + window].reshape(CHUNK_ROWS // 8, 8, lanes)
                for row in range(len(targets)):
                    term = weights_ref[base + row * len(blocks) + column][None] * value
                    totals[row] = term if totals[row] is None else totals[row] + term
            for (ref, index), total in zip(targets, totals):
                ref[(index,) + window] = total.reshape(CHUNK_ROWS, lanes)


def combine(weights, base, inputs, output_count):
    counts = tuple(array.shape[0] for array in inputs)
    shape = jax.ShapeDtypeStruct(inputs[0].shape, jnp.float32)
    moved = sum(counts) + output_count * shape.shape[0]
    block_size = shape.shape[1] * shape.shape[2]
    result = pl.pallas_call(
        functools.partial(combine_kernel, base, counts),
        out_shape=[shape] * output_count,
        in_specs=[VMEM] * (1 + len(inputs)),
        out_specs=[VMEM] * output_count,
        compiler_params=pltpu.CompilerParams(vmem_limit_bytes=SMALL_VMEM),
        cost_estimate=pl.CostEstimate(
            flops=2 * block_size * sum(counts), bytes_accessed=4 * block_size * moved, transcendentals=0
        ),
    )(weights, *inputs)
    return result if output_count > 1 else result[0]


def weights_layout(per_device):
    sizes = [(2, 3), (2, 3), (1, 4), (1, 7), (1, 6), (1, 5)]
    bases = [0]
    for outputs, inputs in sizes:
        bases.append(bases[-1] + outputs * inputs * per_device**2)
    return bases


def weights_kernel(total_energies, per_device, offsets_ref, coupling_ref, occupation_ref, table_ref):
    modes = offsets_ref.shape[0]
    offsets = [offsets_ref[mode] for mode in range(modes)]
    lower = [coupling_ref[mode] * occupation_ref[mode] for mode in range(modes)]
    upper = [coupling_ref[mode] * (occupation_ref[mode] + 1.0) for mode in range(modes)]
    bases = weights_layout(per_device)

    me = lax.axis_index("energy")
    core, y, z = me % 2, (me // 2) % 2, me // 4
    chip = me // 2
    swapped = ((z % 2) == 0) == (y == 1)
    first_far_real = core == 1 - y
    away = 2 * y - 1
    beside, diagonal = chip - away, chip + away

    def energy(at_chip, at_core, index):
        return (2 * at_chip + at_core) * per_device + index

    def own(index):
        return energy(chip, core, index)

    def sibling(index):
        return energy(chip, 1 - core, index)

    def far1(index):
        return energy(chip + 2 * away, 1 - y, index)

    def far2(index):
        return energy(chip - 2 * away, y, index)

    def at(place):
        return lambda index: energy(place, core, index)

    def weight(targets, sources, condition=None):
        def entry(row, column):
            target, source = targets(row), sources(column)
            delta = source - target
            result = jnp.float32(0.0)
            for mode in range(modes):
                result = result + jnp.where(delta == offsets[mode], upper[mode], 0.0)
                result = result + jnp.where(delta == -offsets[mode], lower[mode], 0.0)
            inside = (source >= 0) & (source < total_energies)
            if condition is not None:
                inside = inside & condition
            return jnp.where(inside, result, 0.0)

        return entry

    def same(condition=None):
        def entry(row, column):
            if row != column:
                return jnp.float32(0.0)
            return jnp.float32(1.0) if condition is None else jnp.where(condition, 1.0, 0.0)

        return entry

    def choose(condition, one, other):
        return lambda row, column: jnp.where(condition, one(row, column), other(row, column))

    def none(row, column):
        return jnp.float32(0.0)

    def add(one, other):
        return lambda row, column: one(row, column) + other(row, column)

    real1, real2 = first_far_real, ~first_far_real
    here, there = swapped, ~swapped
    diagonal_at, beside_at = at(diagonal), at(beside)
    sum_row = [weight(diagonal_at, own), weight(diagonal_at, sibling), none]
    far1_row = [none, same(~real1), same(real1)]
    pass_row = [same(), none, none]
    far2_row = [none, same(~real2), same(real2)]
    tables = [
        [
            [choose(swapped, a, b) for a, b in zip(sum_row, far1_row)],
            [choose(swapped, b, a) for a, b in zip(sum_row, far1_row)],
        ],
        [
            [choose(swapped, a, b) for a, b in zip(far2_row, pass_row)],
            [choose(swapped, b, a) for a, b in zip(far2_row, pass_row)],
        ],
        [[weight(beside_at, own), weight(beside_at, sibling), same(there), same(here)]],
        [
            [
                weight(own, own),
                weight(own, sibling),
                same(),
                weight(own, far1, ~real1 & here),
                weight(own, far1, ~real1 & there),
                weight(own, far2, ~real2 & there),
                weight(own, far2, ~real2 & here),
            ]
        ],
        [
            [
                weight(sibling, own),
                weight(sibling, beside_at),
                weight(sibling, far1, real1 & here),
                weight(sibling, far1, real1 & there),
                add(weight(sibling, diagonal_at, here), weight(sibling, far2, real2 & there)),
                add(weight(sibling, diagonal_at, there), weight(sibling, far2, real2 & here)),
            ]
        ],
        [
            [
                weight(own, own),
                weight(own, beside_at),
                weight(own, diagonal_at, here),
                weight(own, diagonal_at, there),
                same(),
            ]
        ],
    ]
    for base, table in zip(bases, tables):
        place = base
        for row in table:
            for row_index in range(per_device):
                for entry in row:
                    for column_index in range(per_device):
                        value = entry(row_index, column_index)
                        table_ref[place] = jnp.full(table_ref.shape[1:], value, jnp.float32)
                        place += 1


def split(value):
    high = value.astype(jnp.bfloat16)
    low = (value - high.astype(jnp.float32)).astype(jnp.bfloat16)
    return high, low


def dot3(left, right, transposed=False):
    numbers = (((1,), (1 if transposed else 0,)), ((), ()))

    def one(a, b):
        return lax.dot_general(a, b, numbers, preferred_element_type=jnp.float32)

    return one(left[0], right[0]) + (one(left[0], right[1]) + one(left[1], right[0]))


def times(left, right):
    real = dot3(left[0], right[0]) - dot3(left[1], right[1])
    imag = dot3(left[0], right[1]) + dot3(left[1], right[0])
    return real, imag


def times_adjoint(left, right):
    real = dot3(left[0], right[0], True) + dot3(left[1], right[1], True)
    imag = dot3(left[1], right[0], True) - dot3(left[0], right[1], True)
    return real, imag


def split_pair(pair):
    return split(pair[0]), split(pair[1])


def bridge_kernel(tiles, mask_ref, hopping_ref, retarded_ref, behind_ref, bridge_ref, *coupled_refs):
    size = hopping_ref.shape[0]
    tile = size // tiles
    column_tile = lax.broadcasted_iota(jnp.int32, (1, size), 1) // tile
    strips = []
    for row in range(tiles):
        strip = jnp.zeros((1, size), jnp.float32)
        for column in range(tiles):
            strip = jnp.where(column_tile == column, mask_ref[row, column].astype(jnp.float32), strip)
        strips.append(hopping_ref[row * tile : (row + 1) * tile, :] * strip)
    masked = split(jnp.concatenate(strips, axis=0))
    for energy in range(retarded_ref.shape[0]):
        coupled = tuple(dot3(split(retarded_ref[energy, part]), masked) for part in range(2))
        for coupled_ref in coupled_refs:
            for part in range(2):
                coupled_ref[energy, part] = coupled[part]
        bridge = times(
            split_pair(coupled), split_pair((behind_ref[energy, 0], behind_ref[energy, 1]))
        )
        for part in range(2):
            bridge_ref[energy, part] = bridge[part]


def row_windows(size):
    cut = size * FIRST_PARTS // PARTS
    return [slice(0, cut), slice(cut, size)]


def source_kernel(pieces, retarded_ref, *refs):
    real_refs, imag_refs, out_ref = refs[:pieces], refs[pieces : 2 * pieces], refs[-1]
    for energy in range(retarded_ref.shape[0]):
        retarded = split_pair((retarded_ref[energy, 0], retarded_ref[energy, 1]))
        real = jnp.concatenate([ref[energy] for ref in real_refs], axis=0)
        imag = jnp.concatenate([ref[energy] for ref in imag_refs], axis=0)
        inner = times(retarded, split_pair((real, imag)))
        outer = times_adjoint(split_pair(inner), retarded)
        for part in range(2):
            out_ref[energy, part] = outer[part]


def piece_kernel(window, bridge_ref, real_ref, imag_ref, out_ref):
    for energy in range(bridge_ref.shape[0]):
        bridge = split_pair((bridge_ref[energy, 0, :, window], bridge_ref[energy, 1, :, window]))
        inner = times(bridge, split_pair((real_ref[energy], imag_ref[energy])))
        for part in range(2):
            out_ref[energy, part] = inner[part]


def imag_half_kernel(window, bridge_ref, imag_ref, total_ref, out_ref):
    for energy in range(bridge_ref.shape[0]):
        imag = split(imag_ref[energy])
        real_share = dot3(split(bridge_ref[energy, 1, :, window]), imag)
        imag_share = dot3(split(bridge_ref[energy, 0, :, window]), imag)
        out_ref[energy, 0] = total_ref[energy, 0] - real_share
        out_ref[energy, 1] = total_ref[energy, 1] + imag_share


def finish_kernel(window, flag_ref, bridge_ref, half_ref, real_ref, source_ref, out_ref):
    @pl.when(flag_ref[0] == 0)
    def _():
        out_ref[...] = source_ref[...]

    @pl.when(flag_ref[0] != 0)
    def _():
        for energy in range(bridge_ref.shape[0]):
            bridge = split_pair((bridge_ref[energy, 0], bridge_ref[energy, 1]))
            real = split(real_ref[energy])
            left = [(high[:, window], low[:, window]) for high, low in bridge]
            inner = tuple(half_ref[energy, part] + dot3(left[part], real) for part in range(2))
            outer = times_adjoint(split_pair(inner), bridge)
            for part in range(2):
                out_ref[energy, part] = source_ref[energy, part] + outer[part]


def advance_kernel(flag_ref, coupled_ref, incoming_ref, source_ref, current_ref, out_ref):
    @pl.when(flag_ref[0] == 0)
    def _():
        out_ref[...] = current_ref[...]

    @pl.when(flag_ref[0] != 0)
    def _():
        for energy in range(coupled_ref.shape[0]):
            coupled = split_pair((coupled_ref[energy, 0], coupled_ref[energy, 1]))
            inner = times(coupled, split_pair((incoming_ref[energy, 0], incoming_ref[energy, 1])))
            outer = times_adjoint(split_pair(inner), coupled)
            for part in range(2):
                out_ref[energy, part] = source_ref[energy, part] + outer[part]


def call(kernel, inputs, specs, outputs, products):
    size = outputs[0].shape[-1]
    return pl.pallas_call(
        kernel,
        out_shape=[jax.ShapeDtypeStruct(array.shape, jnp.float32) for array in outputs],
        in_specs=specs,
        out_specs=[VMEM] * len(outputs),
        compiler_params=pltpu.CompilerParams(vmem_limit_bytes=LARGE_VMEM),
        cost_estimate=pl.CostEstimate(
            flops=6 * products * size**3,
            bytes_accessed=4 * sum(array.size for array in list(inputs) + list(outputs)),
            transcendentals=0,
        ),
    )(*inputs)


def after(value, *gates):
    return lax.optimization_barrier((value,) + gates)[0]


def body(retarded, lesser_prev, hopping, hop_mask, offsets, coupling, occupation):
    devices = lax.axis_size("energy")
    slabs = lax.axis_size("slab")
    per_device = lesser_prev.shape[1]
    assert offsets.shape[0] == 3 and devices % 4 == 0
    bases = weights_layout(per_device)
    weights = pl.pallas_call(
        functools.partial(weights_kernel, per_device * devices, per_device),
        out_shape=jax.ShapeDtypeStruct((bases[-1], 8, 128), jnp.float32),
        in_specs=[SMEM] * 3,
        out_specs=VMEM,
        compiler_params=pltpu.CompilerParams(vmem_limit_bytes=SMALL_VMEM),
    )(offsets, coupling, occupation)

    def permute(value, pairs, name):
        with jax.named_scope(name):
            return lax.ppermute(value, "energy", pairs)

    def to_next_slab(value, name):
        with jax.named_scope(name):
            return lax.ppermute(value, "slab", ahead)

    cores = [(i, i ^ 1) for i in range(devices)]
    across = [(i, i ^ 2) for i in range(devices)]
    first_lines = [(i, i ^ 4) for i in range(devices) if (i ^ 4) < devices]
    second_lines = []
    for i in range(devices):
        other = i + 4 if (i // 4) % 2 == 1 else i - 4
        if 0 <= other < devices:
            second_lines.append((i, other))
    ahead = [(s, (s + 1) % slabs) for s in range(slabs)]

    blocks = retarded[0]
    size = blocks.shape[-1]
    windows = row_windows(size)
    behind = to_next_slab(blocks, "slab_retarded")

    reals, imags, reals_behind, imags_behind = [], [], [], []
    gates = None
    for number, window in enumerate(windows):
        real, imag = lesser_prev[0, :, 0, window], lesser_prev[0, :, 1, window]
        real_sent, imag_own = real, imag
        imag_sibling = permute(imag, cores, f"imag_cores_{number}")
        if gates is not None:
            real_sent = after(real, gates[0])
            imag_own = after(imag, gates[1])
        real_beside = permute(real_sent, across, f"real_across_{number}")
        send1, send2 = combine(weights, bases[0], [imag_own, imag_sibling, real], 2)
        got1 = permute(send1, first_lines, f"lines1a_{number}")
        got2 = permute(send2, second_lines, f"lines1b_{number}")
        if gates is not None:
            real_beside = after(real_beside, gates[2])
        send3, send4 = combine(weights, bases[1], [real_beside, imag_sibling, real], 2)
        got4 = permute(send4, second_lines, f"lines2b_{number}")
        got3 = permute(send3, first_lines, f"lines2a_{number}")
        if number == PIECES - 1:
            got1, behind = lax.optimization_barrier((got1, behind))
        if gates is not None:
            got1 = after(got1, imags_behind[-1])
        beside_sum = combine(weights, bases[2], [imag, imag_sibling, got1, got2], 1)
        imag_beside = permute(beside_sum, across, f"imag_across_{number}")
        self_imag = combine(
            weights, bases[3], [imag, imag_sibling, imag_beside, got1, got2, got3, got4], 1
        )
        real_late = real if gates is None else after(real, self_imag)
        sibling_sum = combine(weights, bases[4], [real_late, real_beside, got1, got2, got3, got4], 1)
        real_sibling = permute(sibling_sum, cores, f"real_cores_{number}")
        if gates is not None:
            got4 = after(got4, reals_behind[-1])
        self_real = combine(weights, bases[5], [real, real_beside, got3, got4, real_sibling], 1)
        gates = (imag_beside, self_imag, self_real)
        imags.append(self_imag)
        reals.append(self_real)
        imags_behind.append(to_next_slab(self_imag, f"slab_imag_{number}"))
        reals_behind.append(to_next_slab(self_real, f"slab_real_{number}"))

    (source,) = call(
        functools.partial(source_kernel, PIECES),
        [blocks] + reals + imags,
        [VMEM] * (1 + 2 * PIECES),
        [blocks],
        16,
    )
    bridge, *coupled = call(
        functools.partial(bridge_kernel, hop_mask.shape[-1]),
        [hop_mask[0], hopping[0], blocks, after(behind, source)],
        [SMEM, VMEM, VMEM, VMEM],
        [blocks] * (2 if slabs > 2 else 1),
        12,
    )
    (total,) = call(
        functools.partial(piece_kernel, windows[0]),
        [bridge, reals_behind[0], imags_behind[0]],
        [VMEM] * 3,
        [blocks],
        8,
    )
    (half,) = call(
        functools.partial(imag_half_kernel, windows[-1]),
        [bridge, imags_behind[-1], total],
        [VMEM] * 3,
        [blocks],
        4,
    )
    position = lax.axis_index("slab")
    turn_flag = (position == 1).astype(jnp.int32).reshape(1)
    (lesser,) = call(
        functools.partial(finish_kernel, windows[-1]),
        [turn_flag, bridge, half, reals_behind[-1], source],
        [SMEM] + [VMEM] * 4,
        [blocks],
        12,
    )
    for turn in range(2, slabs):
        incoming = lax.ppermute(lesser, "slab", ahead)
        (lesser,) = call(
            advance_kernel,
            [(position == turn).astype(jnp.int32).reshape(1), coupled[0], incoming, source, lesser],
            [SMEM] + [VMEM] * 4,
            [blocks],
            16,
        )
    return lesser[None]


def solution(mesh):
    return jax.shard_map(
        body,
        mesh=mesh,
        in_specs=(
            P("slab", "energy", None, None, None),
            P("slab", "energy", None, None, None),
            P("slab", None, None),
            P("slab", None, None),
            P(),
            P(),
            P(),
        ),
        out_specs=P("slab", "energy", None, None, None),
        check_vma=False,
    )
```
